32 devices in a mesh: groups: 2 (over y), sector: 4 (over z), term: 2 (over x), sub: 2 (over core).
Axes of the slice: x: 2, y: 2, z: 4, core: 2. Of those that a mesh axis runs over, the one named last changes fastest.
Arguments:
- wavefunction: bfloat16 [8, 4, 512, 512], P(('groups', 'sector'), 'term', 'sub'), parts along dimension 0, may hold values from -6 to 6
- left_env: bfloat16 [2, 8, 512, 512], P('term', ('groups', 'sector')), parts along dimension 1, may hold values from -0.1875 to 0.1875
- right_env: bfloat16 [2, 8, 512, 512], P('term', ('groups', 'sector')), parts along dimension 1, may hold values from -0.25 to 0.25
- left_dims: int32 [8], P('groups'), parts along dimension 0, may hold values from 128 to 512
- right_dims: int32 [8], P('groups'), parts along dimension 0, may hold values from 128 to 512
Outputs:
- product: bfloat16 [8, 4, 512, 512], P(('groups', 'sector'), 'term', 'sub'), parts along dimension 0
The draws below stay inside these ranges and needn't reach their ends.
There are 2 independent parts, one for each index of `groups`. The reference program is written for one: setup_inputs(seed, part) draws one part's arguments, and reference() takes and returns one part's arrays. A program takes and returns all parts, laid end to end along the dimension named above; each array names one. Nothing has to cross between parts.
All inputs are finite; a program needn't handle non-finite values.
Results may differ from the reference program's by a relative error of at most 0.0051.
Values may be sent and summed in bfloat16 or wider, within the bound.
No kernel may reach another device: no remote copies, remote signals or barrier semaphores. Data moves between devices by JAX's collectives and lax.ppermute only.
A program may use at most 64 MiB of HBM per device.

```python
import jax
import jax.numpy as jnp
from jax import lax

BLOCK = 512
SECTORS = 4
TERMS = 2


def touch_ends(result, rng, smallest, largest):
    extent = result.shape
    place = [jax.random.randint(jax.random.fold_in(rng, axis), (), 0, extent[axis]) for axis in range(len(extent))]
    result = result.at[tuple(place)].set(smallest)
    longest = extent.index(max(extent))
    place[longest] = (place[longest] + 1) % extent[longest]
    return result.at[tuple(place)].set(largest)


def shard_levels(own_key, dims, cuts, least, top_value):
    gain, own = 1.0, jax.random.fold_in(own_key, 6)
    for dim, blocks in cuts:
        draws = jnp.exp(jax.random.uniform(jax.random.fold_in(own, dim), (blocks,), jnp.float32, least / len(cuts), top_value / len(cuts)))
        gain = gain * jnp.repeat(draws, dims[dim] // blocks).reshape([-1 if axis == dim else 1 for axis in range(len(dims))])
    return gain


def gaussian(own_key, dims, spread, bound, split=(), kind=jnp.bfloat16):
    array = spread * jax.random.normal(own_key, dims, jnp.float32)
    if split:
        array = array * shard_levels(own_key, dims, split, -0.22, 0.18)
    return jnp.clip(array, -bound, bound).astype(kind)


def setup_inputs(seed: int = 0, part: int = 0) -> dict:
    key_list = jax.random.split(jax.random.key(seed), 6)
    part_splits = jax.random.split(jax.random.fold_in(key_list[5], part), 6)
    wavefunction = gaussian(part_splits[0], (SECTORS, SECTORS, BLOCK, BLOCK), 1.0, 6.0, ((0, 4), (1, 2), (2, 2)))
    left_env = gaussian(part_splits[1], (TERMS, SECTORS, BLOCK, BLOCK), (TERMS * BLOCK) ** -0.5, 0.1875, ((0, 2), (1, 4)))
    right_env = gaussian(part_splits[2], (TERMS, SECTORS, BLOCK, BLOCK), BLOCK ** -0.5, 0.25, ((0, 2), (1, 4)))
    left_dims = touch_ends(jax.random.randint(part_splits[3], (SECTORS,), BLOCK // 4, BLOCK + 1), jax.random.fold_in(part_splits[3], 1), BLOCK // 4, BLOCK).astype(jnp.int32)
    right_dims = touch_ends(jax.random.randint(part_splits[4], (SECTORS,), BLOCK // 4, BLOCK + 1), jax.random.fold_in(part_splits[4], 1), BLOCK // 4, BLOCK).astype(jnp.int32)
    return dict(wavefunction=wavefunction, left_env=left_env, right_env=right_env, left_dims=left_dims, right_dims=right_dims)


def reference(wavefunction, left_env, right_env, left_dims, right_dims):
    states = jnp.arange(BLOCK, dtype=jnp.int32)
    row_live = states[None, :] < left_dims[:, None]
    col_live = states[None, :] < right_dims[:, None]
    masked = jnp.where(row_live[None, :, :, None] & col_live[:, None, None, :], wavefunction, jnp.zeros((), wavefunction.dtype))
    right_wide = right_env.astype(jnp.float32)

    def one_sector(index):
        blocks = lax.dynamic_index_in_dim(masked, index, 1, keepdims=False)
        left_part = lax.dynamic_index_in_dim(left_env, index, 1, keepdims=False)
        moved = jnp.einsum('bkj,wbcj->wbkc', blocks.astype(jnp.float32), right_wide).astype(jnp.bfloat16)
        summed = jnp.einsum('wrk,wbkc->brc', left_part.astype(jnp.float32), moved.astype(jnp.float32))
        rows_ok = lax.dynamic_index_in_dim(row_live, index, 0, keepdims=False)
        summed = jnp.where(rows_ok[None, :, None] & col_live[:, None, :], summed, jnp.zeros((), jnp.float32))
        return summed.astype(jnp.bfloat16)

    return lax.map(one_sector, jnp.arange(SECTORS, dtype=jnp.int32))
```

```python
import jax
import jax.numpy as jnp
from jax import lax
from jax.sharding import PartitionSpec as P

LINE = ("sector", "term", "sub")
F32 = jnp.float32
BF16 = jnp.bfloat16


def masked_envs(left_env, right_env, left_dims, right_dims, sector_pos):
    states = jnp.arange(left_env.shape[-1], dtype=jnp.int32)
    left_live = states < lax.dynamic_index_in_dim(left_dims, sector_pos, 0, keepdims=False)
    right_live = states < lax.dynamic_index_in_dim(right_dims, sector_pos, 0, keepdims=False)
    left = jnp.where(left_live[:, None] & left_live[None, :], left_env[0, 0], jnp.zeros((), left_env.dtype))
    right = jnp.where(right_live[:, None] & right_live[None, :], right_env[0, 0], jnp.zeros((), right_env.dtype))
    return left, right


def two_by_four(wavefunction, left_env, right_env, left_dims, right_dims):
    z, t, u = (lax.axis_index(name) for name in LINE)
    sectors, terms, subs = (lax.axis_size(name) for name in LINE)
    half = wavefunction.shape[2]
    home = (z // 2) == t
    odd = (z & 1) == 1

    def index(zz, tt, uu):
        return (zz * terms + tt) * subs + uu

    def permute(value, target):
        pairs = []
        for zz in range(sectors):
            for tt in range(terms):
                for uu in range(subs):
                    place = target(zz, tt, uu)
                    if place is not None:
                        pairs.append((index(zz, tt, uu), index(*place)))
        return lax.ppermute(value, LINE, pairs)

    def over_term(value):
        return permute(value, lambda zz, tt, uu: (zz, 1 - tt, uu))

    def over_core(value):
        return permute(value, lambda zz, tt, uu: (zz, tt, 1 - uu))

    def from_home(value, flip):
        return permute(value, lambda zz, tt, uu: (zz ^ flip, tt, uu) if zz // 2 == tt else None)

    def from_away(value, flip):
        return permute(value, lambda zz, tt, uu: (zz ^ flip, tt, uu) if zz // 2 != tt else None)

    own_same = jnp.where(odd, wavefunction[0, 1], wavefunction[0, 0])
    own_flip = jnp.where(odd, wavefunction[0, 0], wavefunction[0, 1])
    other_same = over_term(own_same)
    other_flip = over_term(own_flip)
    left, right = masked_envs(left_env, right_env, left_dims, right_dims, z)
    rows = lax.dynamic_slice_in_dim(left, u * half, half, 0)
    left_mine = lax.dynamic_slice_in_dim(rows, u * half, half, 1)
    left_theirs = lax.dynamic_slice_in_dim(rows, (1 - u) * half, half, 1)

    def contract(block):
        return lax.dot_general(block, right, (((1,), (1,)), ((), ())), preferred_element_type=F32).astype(BF16)

    def apply_left(mine, theirs):
        return jnp.dot(left_mine, mine, preferred_element_type=F32) + jnp.dot(
            left_theirs, theirs, preferred_element_type=F32
        )

    moved_own_same = contract(own_same)
    moved_own_flip = contract(own_flip)
    early_same = from_away(moved_own_same, 2)
    early_flip = from_away(moved_own_flip, 3)
    moved_other_same = contract(other_same)
    late_same = from_home(moved_other_same, 2)
    moved_other_flip = contract(other_flip)
    late_flip = from_home(moved_other_flip, 3)
    near = permute(jnp.where(home, moved_own_flip, moved_other_flip), lambda zz, tt, uu: (zz ^ 1, tt, uu))

    away1 = jnp.where(home, early_same, moved_other_same)
    away1_sent = over_term(apply_left(away1, over_core(away1)).astype(BF16))
    away2 = jnp.where(home, early_flip, near)
    away2_sent = over_term(apply_left(away2, over_core(away2)).astype(BF16))
    kept1 = jnp.where(home, moved_own_same, late_same)
    out1 = (apply_left(kept1, over_core(kept1)) + away1_sent.astype(F32)).astype(BF16)
    kept2 = jnp.where(home, near, late_flip)
    out2 = (apply_left(kept2, over_core(kept2)) + away2_sent.astype(F32)).astype(BF16)
    return jnp.stack([jnp.where(odd, out2, out1), jnp.where(odd, out1, out2)])[None]


def any_size(wavefunction, left_env, right_env, left_dims, right_dims):
    z, t, u = (lax.axis_index(name) for name in LINE)
    half = wavefunction.shape[2]
    left, right = masked_envs(left_env, right_env, left_dims, right_dims, z)
    rows = lax.dynamic_slice_in_dim(left, u * half, half, 0)
    blocks = lax.all_gather(wavefunction[0], "term", axis=0, tiled=True)
    moved = jnp.einsum("akj,cj->akc", blocks, right, preferred_element_type=F32).astype(BF16)
    arrived = lax.all_to_all(moved, "sector", split_axis=0, concat_axis=0, tiled=True)
    both = lax.all_gather(arrived, "sub", axis=1, tiled=True)
    partial = jnp.einsum("rk,bkc->brc", rows, both, preferred_element_type=F32)
    return lax.psum_scatter(partial, "term", scatter_dimension=0, tiled=True).astype(BF16)[None]


def solution(mesh):
    sizes = tuple(mesh.shape[name] for name in LINE)
    return jax.shard_map(
        two_by_four if sizes == (4, 2, 2) else any_size,
        mesh=mesh,
        in_specs=(
            P(("groups", "sector"), "term", "sub", None),
            P("term", ("groups", "sector"), None, None),
            P("term", ("groups", "sector"), None, None),
            P("groups"),
            P("groups"),
        ),
        out_specs=P(("groups", "sector"), "term", "sub", None),
        check_vma=False,
    )
```

```python
import jax
import jax.numpy as jnp
from jax import lax
from jax.sharding import PartitionSpec as P

LINE = ("sector", "term", "sub")
F32 = jnp.float32
BF16 = jnp.bfloat16


def masked_envs(left_env, right_env, left_dims, right_dims, sector_pos):
    states = jnp.arange(left_env.shape[-1], dtype=jnp.int32)
    left_live = states < lax.dynamic_index_in_dim(left_dims, sector_pos, 0, keepdims=False)
    right_live = states < lax.dynamic_index_in_dim(right_dims, sector_pos, 0, keepdims=False)
    left = jnp.where(left_live[:, None] & left_live[None, :], left_env[0, 0], jnp.zeros((), left_env.dtype))
    right = jnp.where(right_live[:, None] & right_live[None, :], right_env[0, 0], jnp.zeros((), right_env.dtype))
    return left, right


def take(values, position):
    places = jnp.arange(values.shape[0], dtype=jnp.int32)
    return jnp.sum(jnp.where(places == position, values, 0))


def contract(block, right):
    return lax.dot_general(block, right, (((1,), (1,)), ((), ())), preferred_element_type=F32).astype(BF16)


def two_by_four(wavefunction, left_env, right_env, left_dims, right_dims):
    z, t, u = (lax.axis_index(name) for name in LINE)
    sectors, terms, subs = (lax.axis_size(name) for name in LINE)
    half, width = wavefunction.shape[2:]
    states = jnp.arange(width, dtype=jnp.int32)
    at_home = (z // 2) == t
    odd = z & 1

    def index(zz, tt, uu):
        return (zz * terms + tt) * subs + uu

    def permute(value, home, away):
        pairs = []
        for zz in range(sectors):
            for tt in range(terms):
                flip_sector, flip_term, flip_sub = home if zz // 2 == tt else away
                for uu in range(subs):
                    pairs.append((index(zz, tt, uu), index(zz ^ flip_sector, tt ^ flip_term, uu ^ flip_sub)))
        return lax.ppermute(value, LINE, pairs)

    def over_term(value):
        return permute(value, (0, 1, 0), (0, 1, 0))

    def over_core(value):
        return permute(value, (0, 0, 1), (0, 0, 1))

    own_same = lax.dynamic_index_in_dim(wavefunction[0], odd, 0, keepdims=False)
    own_flip = lax.dynamic_index_in_dim(wavefunction[0], 1 - odd, 0, keepdims=False)
    other_same = over_term(own_same)
    other_flip = over_term(own_flip)

    live = states < take(right_dims, z)
    right = jnp.where(live[:, None] & live[None, :], right_env[0, 0], jnp.zeros((), BF16))
    same_first = permute(contract(own_same, right), (0, 0, 0), (2, 1, 0))
    flip_first = permute(contract(own_flip, right), (1, 0, 0), (3, 1, 0))
    same_second = permute(contract(other_same, right), (2, 0, 0), (0, 1, 0))
    moved_last = contract(other_flip, right)
    flip_second = permute(moved_last, (3, 0, 0), (1, 1, 0))

    later_u, moved_last = lax.optimization_barrier((u, moved_last))
    own_rows = lax.dynamic_slice_in_dim(left_env[0, 0], later_u * half, half, 0)
    other_rows = over_term(own_rows)
    count = take(left_dims, z)
    rows_live = (u * half + states[:half]) < count
    cols_live = states < count
    lefts = []
    for rows in (jnp.where(at_home, own_rows, other_rows), jnp.where(at_home, other_rows, own_rows)):
        rows = jnp.where(rows_live[:, None] & cols_live[None, :], rows, jnp.zeros((), BF16))
        lefts.append([lax.dynamic_slice_in_dim(rows, part * half, half, 1) for part in (u, 1 - u)])

    def apply_left(left, mine):
        return jnp.dot(left[0], mine, preferred_element_type=F32) + jnp.dot(
            left[1], over_core(mine), preferred_element_type=F32
        )

    same = apply_left(lefts[0], same_first) + apply_left(lefts[1], same_second)
    flip = apply_left(lefts[0], flip_first) + apply_left(lefts[1], flip_second)
    same, flip = same.astype(BF16), flip.astype(BF16)
    return jnp.stack([jnp.where(odd == 1, flip, same), jnp.where(odd == 1, same, flip)])[None]


def any_size(wavefunction, left_env, right_env, left_dims, right_dims):
    z, t, u = (lax.axis_index(name) for name in LINE)
    half = wavefunction.shape[2]
    left, right = masked_envs(left_env, right_env, left_dims, right_dims, z)
    rows = lax.dynamic_slice_in_dim(left, u * half, half, 0)
    blocks = lax.all_gather(wavefunction[0], "term", axis=0, tiled=True)
    moved = jnp.einsum("akj,cj->akc", blocks, right, preferred_element_type=F32).astype(BF16)
    arrived = lax.all_to_all(moved, "sector", split_axis=0, concat_axis=0, tiled=True)
    both = lax.all_gather(arrived, "sub", axis=1, tiled=True)
    partial = jnp.einsum("rk,bkc->brc", rows, both, preferred_element_type=F32)
    return lax.psum_scatter(partial, "term", scatter_dimension=0, tiled=True).astype(BF16)[None]


def solution(mesh):
    sizes = tuple(mesh.shape[name] for name in LINE)
    return jax.shard_map(
        two_by_four if sizes == (4, 2, 2) else any_size,
        mesh=mesh,
        in_specs=(
            P(("groups", "sector"), "term", "sub", None),
            P("term", ("groups", "sector"), None, None),
            P("term", ("groups", "sector"), None, None),
            P("groups"),
            P("groups"),
        ),
        out_specs=P(("groups", "sector"), "term", "sub", None),
        check_vma=False,
    )
```

```python
import jax
import jax.numpy as jnp
from jax import lax
from jax.sharding import PartitionSpec as P

LINE = ("sector", "term", "sub")
F32 = jnp.float32
BF16 = jnp.bfloat16


def masked_envs(left_env, right_env, left_dims, right_dims, sector_pos):
    states = jnp.arange(left_env.shape[-1], dtype=jnp.int32)
    left_live = states < lax.dynamic_index_in_dim(left_dims, sector_pos, 0, keepdims=False)
    right_live = states < lax.dynamic_index_in_dim(right_dims, sector_pos, 0, keepdims=False)
    left = jnp.where(left_live[:, None] & left_live[None, :], left_env[0, 0], jnp.zeros((), left_env.dtype))
    right = jnp.where(right_live[:, None] & right_live[None, :], right_env[0, 0], jnp.zeros((), right_env.dtype))
    return left, right


def take(values, position):
    places = jnp.arange(values.shape[0], dtype=jnp.int32)
    return jnp.sum(jnp.where(places == position, values, 0))


def contract(block, right):
    return lax.dot_general(block, right, (((1,), (1,)), ((), ())), preferred_element_type=F32).astype(BF16)


def two_by_four(wavefunction, left_env, right_env, left_dims, right_dims):
    z, t, u = (lax.axis_index(name) for name in LINE)
    sectors, terms, subs = (lax.axis_size(name) for name in LINE)
    half, width = wavefunction.shape[2:]
    states = jnp.arange(width, dtype=jnp.int32)
    at_home = (z // 2) == t
    odd = z & 1

    def index(zz, tt, uu):
        return (zz * terms + tt) * subs + uu

    def permute(value, home, away):
        pairs = []
        for zz in range(sectors):
            for tt in range(terms):
                flip_sector, flip_term, flip_sub = home if zz // 2 == tt else away
                for uu in range(subs):
                    pairs.append((index(zz, tt, uu), index(zz ^ flip_sector, tt ^ flip_term, uu ^ flip_sub)))
        return lax.ppermute(value, LINE, pairs)

    def over_term(value):
        return permute(value, (0, 1, 0), (0, 1, 0))

    def over_core(value):
        return permute(value, (0, 0, 1), (0, 0, 1))

    own_same = lax.dynamic_index_in_dim(wavefunction[0], odd, 0, keepdims=False)
    own_flip = lax.dynamic_index_in_dim(wavefunction[0], 1 - odd, 0, keepdims=False)
    other_same = over_term(own_same)
    other_flip = over_term(own_flip)

    live = states < take(right_dims, z)
    right = jnp.where(live[:, None] & live[None, :], right_env[0, 0], jnp.zeros((), BF16))
    same_first = permute(contract(own_same, right), (0, 0, 0), (2, 1, 0))
    flip_first = permute(contract(own_flip, right), (1, 0, 0), (3, 1, 0))
    moved_same = contract(other_same, right)
    same_second = permute(moved_same, (2, 0, 0), (0, 1, 0))
    other_flip, moved_same = lax.optimization_barrier((other_flip, moved_same))
    moved_last = contract(other_flip, right)
    flip_second = permute(moved_last, (3, 0, 0), (1, 1, 0))

    later_u, moved_last = lax.optimization_barrier((u, moved_last))
    own_rows = lax.dynamic_slice_in_dim(left_env[0, 0], later_u * half, half, 0)
    other_rows = over_term(own_rows)
    count = take(left_dims, z)
    rows_live = (u * half + states[:half]) < count
    cols_live = states < count
    lefts = []
    for rows in (jnp.where(at_home, own_rows, other_rows), jnp.where(at_home, other_rows, own_rows)):
        rows = jnp.where(rows_live[:, None] & cols_live[None, :], rows, jnp.zeros((), BF16))
        lefts.append([lax.dynamic_slice_in_dim(rows, part * half, half, 1) for part in (u, 1 - u)])

    def apply_left(left, mine):
        return jnp.dot(left[0], mine, preferred_element_type=F32) + jnp.dot(
            left[1], over_core(mine), preferred_element_type=F32
        )

    same = apply_left(lefts[0], same_first) + apply_left(lefts[1], same_second)
    flip = apply_left(lefts[0], flip_first) + apply_left(lefts[1], flip_second)
    same, flip = same.astype(BF16), flip.astype(BF16)
    return jnp.stack([jnp.where(odd == 1, flip, same), jnp.where(odd == 1, same, flip)])[None]


def any_size(wavefunction, left_env, right_env, left_dims, right_dims):
    z, t, u = (lax.axis_index(name) for name in LINE)
    half = wavefunction.shape[2]
    left, right = masked_envs(left_env, right_env, left_dims, right_dims, z)
    rows = lax.dynamic_slice_in_dim(left, u * half, half, 0)
    blocks = lax.all_gather(wavefunction[0], "term", axis=0, tiled=True)
    moved = jnp.einsum("akj,cj->akc", blocks, right, preferred_element_type=F32).astype(BF16)
    arrived = lax.all_to_all(moved, "sector", split_axis=0, concat_axis=0, tiled=True)
    both = lax.all_gather(arrived, "sub", axis=1, tiled=True)
    partial = jnp.einsum("rk,bkc->brc", rows, both, preferred_element_type=F32)
    return lax.psum_scatter(partial, "term", scatter_dimension=0, tiled=True).astype(BF16)[None]


def solution(mesh):
    sizes = tuple(mesh.shape[name] for name in LINE)
    return jax.shard_map(
        two_by_four if sizes == (4, 2, 2) else any_size,
        mesh=mesh,
        in_specs=(
            P(("groups", "sector"), "term", "sub", None),
            P("term", ("groups", "sector"), None, None),
            P("term", ("groups", "sector"), None, None),
            P("groups"),
            P("groups"),
        ),
        out_specs=P(("groups", "sector"), "term", "sub", None),
        check_vma=False,
    )
```

```python
import jax
import jax.numpy as jnp
from jax import lax
from jax.sharding import PartitionSpec as P

LINE = ("sector", "term", "sub")
F32 = jnp.float32
BF16 = jnp.bfloat16


def masked_envs(left_env, right_env, left_dims, right_dims, sector_pos):
    states = jnp.arange(left_env.shape[-1], dtype=jnp.int32)
    left_live = states < lax.dynamic_index_in_dim(left_dims, sector_pos, 0, keepdims=False)
    right_live = states < lax.dynamic_index_in_dim(right_dims, sector_pos, 0, keepdims=False)
    left = jnp.where(left_live[:, None] & left_live[None, :], left_env[0, 0], jnp.zeros((), left_env.dtype))
    right = jnp.where(right_live[:, None] & right_live[None, :], right_env[0, 0], jnp.zeros((), right_env.dtype))
    return left, right


def live_states(dims, sector, states):
    places = jnp.arange(dims.shape[0], dtype=jnp.int32)
    return jnp.any((places[:, None] == sector) & (states[None, :] < dims[:, None]), axis=0)


def contract(block, right):
    return lax.dot_general(block, right, (((1,), (1,)), ((), ())), preferred_element_type=F32).astype(BF16)


def two_by_four(wavefunction, left_env, right_env, left_dims, right_dims):
    z, t, u = (lax.axis_index(name) for name in LINE)
    sectors, terms, subs = (lax.axis_size(name) for name in LINE)
    half, width = wavefunction.shape[2:]
    states = jnp.arange(width, dtype=jnp.int32)
    at_home = (z // 2) == t
    odd = z & 1

    def index(zz, tt, uu):
        return (zz * terms + tt) * subs + uu

    def permute(value, home, away):
        pairs = []
        for zz in range(sectors):
            for tt in range(terms):
                flip_sector, flip_term, flip_sub = home if zz // 2 == tt else away
                for uu in range(subs):
                    pairs.append((index(zz, tt, uu), index(zz ^ flip_sector, tt ^ flip_term, uu ^ flip_sub)))
        return lax.ppermute(value, LINE, pairs)

    def over_term(value):
        return permute(value, (0, 1, 0), (0, 1, 0))

    def over_core(value):
        return permute(value, (0, 0, 1), (0, 0, 1))

    own_same = lax.dynamic_index_in_dim(wavefunction[0], odd, 0, keepdims=False)
    own_flip = lax.dynamic_index_in_dim(wavefunction[0], 1 - odd, 0, keepdims=False)
    other_same = over_term(own_same)
    other_flip = over_term(own_flip)

    live = live_states(right_dims, z, states)
    right = jnp.where(live[:, None] & live[None, :], right_env[0, 0], jnp.zeros((), BF16))
    same_first = permute(contract(own_same, right), (0, 0, 0), (2, 1, 0))
    moved_same = contract(other_same, right)
    same_second = permute(moved_same, (2, 0, 0), (0, 1, 0))
    own_flip, other_flip, moved_same = lax.optimization_barrier((own_flip, other_flip, moved_same))
    flip_first = permute(contract(own_flip, right), (1, 0, 0), (3, 1, 0))
    moved_last = contract(other_flip, right)
    flip_second = permute(moved_last, (3, 0, 0), (1, 1, 0))

    later_u, moved_last = lax.optimization_barrier((u, moved_last))
    own_rows = lax.dynamic_slice_in_dim(left_env[0, 0], later_u * half, half, 0)
    other_rows = over_term(own_rows)
    cols_live = live_states(left_dims, z, states)
    rows_live = lax.dynamic_slice_in_dim(cols_live, u * half, half)
    lefts = []
    for rows in (jnp.where(at_home, own_rows, other_rows), jnp.where(at_home, other_rows, own_rows)):
        rows = jnp.where(rows_live[:, None] & cols_live[None, :], rows, jnp.zeros((), BF16))
        lefts.append([lax.dynamic_slice_in_dim(rows, part * half, half, 1) for part in (u, 1 - u)])

    def apply_left(left, mine):
        return jnp.dot(left[0], mine, preferred_element_type=F32) + jnp.dot(
            left[1], over_core(mine), preferred_element_type=F32
        )

    same = apply_left(lefts[0], same_first)
    flip = apply_left(lefts[0], flip_first)
    same = (same + apply_left(lefts[1], same_second)).astype(BF16)
    flip, flip_second, same = lax.optimization_barrier((flip, flip_second, same))
    flip = (flip + apply_left(lefts[1], flip_second)).astype(BF16)
    product = jnp.zeros((1, 2, half, width), BF16)
    product = lax.dynamic_update_slice(product, same[None, None], (0, odd, 0, 0))
    return lax.dynamic_update_slice(product, flip[None, None], (0, 1 - odd, 0, 0))


def any_size(wavefunction, left_env, right_env, left_dims, right_dims):
    z, t, u = (lax.axis_index(name) for name in LINE)
    half = wavefunction.shape[2]
    left, right = masked_envs(left_env, right_env, left_dims, right_dims, z)
    rows = lax.dynamic_slice_in_dim(left, u * half, half, 0)
    blocks = lax.all_gather(wavefunction[0], "term", axis=0, tiled=True)
    moved = jnp.einsum("akj,cj->akc", blocks, right, preferred_element_type=F32).astype(BF16)
    arrived = lax.all_to_all(moved, "sector", split_axis=0, concat_axis=0, tiled=True)
    both = lax.all_gather(arrived, "sub", axis=1, tiled=True)
    partial = jnp.einsum("rk,bkc->brc", rows, both, preferred_element_type=F32)
    return lax.psum_scatter(partial, "term", scatter_dimension=0, tiled=True).astype(BF16)[None]


def solution(mesh):
    sizes = tuple(mesh.shape[name] for name in LINE)
    return jax.shard_map(
        two_by_four if sizes == (4, 2, 2) else any_size,
        mesh=mesh,
        in_specs=(
            P(("groups", "sector"), "term", "sub", None),
            P("term", ("groups", "sector"), None, None),
            P("term", ("groups", "sector"), None, None),
            P("groups"),
            P("groups"),
        ),
        out_specs=P(("groups", "sector"), "term", "sub", None),
        check_vma=False,
    )
```

```python
import jax
import jax.numpy as jnp
from jax import lax
from jax.sharding import PartitionSpec as P

LINE = ("sector", "term", "sub")
F32 = jnp.float32
BF16 = jnp.bfloat16


def masked_envs(left_env, right_env, left_dims, right_dims, sector_pos):
    states = jnp.arange(left_env.shape[-1], dtype=jnp.int32)
    left_live = states < lax.dynamic_index_in_dim(left_dims, sector_pos, 0, keepdims=False)
    right_live = states < lax.dynamic_index_in_dim(right_dims, sector_pos, 0, keepdims=False)
    left = jnp.where(left_live[:, None] & left_live[None, :], left_env[0, 0], jnp.zeros((), left_env.dtype))
    right = jnp.where(right_live[:, None] & right_live[None, :], right_env[0, 0], jnp.zeros((), right_env.dtype))
    return left, right


def live_states(dims, sector, states):
    places = jnp.arange(dims.shape[0], dtype=jnp.int32)
    return jnp.any((places[:, None] == sector) & (states[None, :] < dims[:, None]), axis=0)


def contract(block, right):
    return lax.dot_general(block, right, (((1,), (1,)), ((), ())), preferred_element_type=F32).astype(BF16)


def two_by_four(wavefunction, left_env, right_env, left_dims, right_dims):
    z, t, u = (lax.axis_index(name) for name in LINE)
    sectors, terms, subs = (lax.axis_size(name) for name in LINE)
    half, width = wavefunction.shape[2:]
    states = jnp.arange(width, dtype=jnp.int32)
    at_home = (z // 2) == t
    odd = z & 1

    def index(zz, tt, uu):
        return (zz * terms + tt) * subs + uu

    def permute(value, home, away):
        pairs = []
        for zz in range(sectors):
            for tt in range(terms):
                flips = home if zz // 2 == tt else away
                if flips is None:
                    continue
                flip_sector, flip_term, flip_sub = flips
                for uu in range(subs):
                    pairs.append((index(zz, tt, uu), index(zz ^ flip_sector, tt ^ flip_term, uu ^ flip_sub)))
        return lax.ppermute(value, LINE, pairs)

    def over_term(value):
        return permute(value, (0, 1, 0), (0, 1, 0))

    def over_core(value):
        return permute(value, (0, 0, 1), (0, 0, 1))

    own_same = lax.dynamic_index_in_dim(wavefunction[0], odd, 0, keepdims=False)
    own_flip = lax.dynamic_index_in_dim(wavefunction[0], 1 - odd, 0, keepdims=False)
    other_same = permute(own_same, (0, 1, 0), (0, 1, 0))
    second_flip = own_flip
    other_flip = permute(second_flip, (0, 1, 0), (0, 1, 0))
    live = live_states(right_dims, z, states)
    right = jnp.where(live[:, None] & live[None, :], right_env[0, 0], jnp.zeros((), BF16))
    moved_first = contract(own_same, right)
    same_first = permute(moved_first, (0, 0, 0), (2, 1, 0))
    other_same, _ = lax.optimization_barrier((other_same, moved_first))
    moved_same = contract(other_same, right)
    same_second = permute(moved_same, (2, 0, 0), (0, 1, 0))
    later_u = u
    later_u, _ = lax.optimization_barrier((later_u, moved_same))
    own_rows = lax.dynamic_slice_in_dim(left_env[0, 0], later_u * half, half, 0)
    other_rows = over_term(own_rows)
    early_flip, own_rows = lax.optimization_barrier((own_flip, own_rows))
    early_flip, _ = lax.optimization_barrier((early_flip, moved_same))
    moved_flip = contract(early_flip, right)
    flip_first = permute(moved_flip, (1, 0, 0), (3, 1, 0))
    other_flip, _, _ = lax.optimization_barrier((other_flip, moved_same, moved_flip))
    moved_last = contract(other_flip, right)
    flip_second = permute(moved_last, (3, 0, 0), (1, 1, 0))
    cols_live = live_states(left_dims, z, states)
    rows_live = lax.dynamic_slice_in_dim(cols_live, u * half, half)
    lefts = []
    for rows in (jnp.where(at_home, own_rows, other_rows), jnp.where(at_home, other_rows, own_rows)):
        rows = jnp.where(rows_live[:, None] & cols_live[None, :], rows, jnp.zeros((), BF16))
        lefts.append([lax.dynamic_slice_in_dim(rows, part * half, half, 1) for part in (u, 1 - u)])

    def apply_left(left, mine):
        return jnp.dot(left[0], mine, preferred_element_type=F32) + jnp.dot(
            left[1], over_core(mine), preferred_element_type=F32
        )

    same = apply_left(lefts[0], same_first)
    flip = apply_left(lefts[0], flip_first)
    same = (same + apply_left(lefts[1], same_second)).astype(BF16)
    flip, flip_second, same = lax.optimization_barrier((flip, flip_second, same))
    flip = (flip + apply_left(lefts[1], flip_second)).astype(BF16)
    product = jnp.zeros((1, 2, half, width), BF16)
    product = lax.dynamic_update_slice(product, same[None, None], (0, odd, 0, 0))
    return lax.dynamic_update_slice(product, flip[None, None], (0, 1 - odd, 0, 0))


def any_size(wavefunction, left_env, right_env, left_dims, right_dims):
    z, t, u = (lax.axis_index(name) for name in LINE)
    half = wavefunction.shape[2]
    left, right = masked_envs(left_env, right_env, left_dims, right_dims, z)
    rows = lax.dynamic_slice_in_dim(left, u * half, half, 0)
    blocks = lax.all_gather(wavefunction[0], "term", axis=0, tiled=True)
    moved = jnp.einsum("akj,cj->akc", blocks, right, preferred_element_type=F32).astype(BF16)
    arrived = lax.all_to_all(moved, "sector", split_axis=0, concat_axis=0, tiled=True)
    both = lax.all_gather(arrived, "sub", axis=1, tiled=True)
    partial = jnp.einsum("rk,bkc->brc", rows, both, preferred_element_type=F32)
    return lax.psum_scatter(partial, "term", scatter_dimension=0, tiled=True).astype(BF16)[None]


def solution(mesh):
    sizes = tuple(mesh.shape[name] for name in LINE)
    return jax.shard_map(
        two_by_four if sizes == (4, 2, 2) else any_size,
        mesh=mesh,
        in_specs=(
            P(("groups", "sector"), "term", "sub", None),
            P("term", ("groups", "sector"), None, None),
            P("term", ("groups", "sector"), None, None),
            P("groups"),
            P("groups"),
        ),
        out_specs=P(("groups", "sector"), "term", "sub", None),
        check_vma=False,
    )
```

```python
import jax
import jax.numpy as jnp
from jax import lax
from jax.sharding import PartitionSpec as P

LINE = ("sector", "term", "sub")
F32 = jnp.float32
BF16 = jnp.bfloat16


def masked_envs(left_env, right_env, left_dims, right_dims, sector_pos):
    states = jnp.arange(left_env.shape[-1], dtype=jnp.int32)
    left_live = states < lax.dynamic_index_in_dim(left_dims, sector_pos, 0, keepdims=False)
    right_live = states < lax.dynamic_index_in_dim(right_dims, sector_pos, 0, keepdims=False)
    left = jnp.where(left_live[:, None] & left_live[None, :], left_env[0, 0], jnp.zeros((), left_env.dtype))
    right = jnp.where(right_live[:, None] & right_live[None, :], right_env[0, 0], jnp.zeros((), right_env.dtype))
    return left, right


def live_states(dims, sector, states):
    places = jnp.arange(dims.shape[0], dtype=jnp.int32)
    return jnp.any((places[:, None] == sector) & (states[None, :] < dims[:, None]), axis=0)


def contract(block, right):
    return lax.dot_general(block, right, (((1,), (1,)), ((), ())), preferred_element_type=F32).astype(BF16)


def two_by_four(wavefunction, left_env, right_env, left_dims, right_dims):
    z, t, u = (lax.axis_index(name) for name in LINE)
    sectors, terms, subs = (lax.axis_size(name) for name in LINE)
    half, width = wavefunction.shape[2:]
    states = jnp.arange(width, dtype=jnp.int32)
    at_home = (z // 2) == t
    odd = z & 1

    def index(zz, tt, uu):
        return (zz * terms + tt) * subs + uu

    def permute(value, home, away):
        pairs = []
        for zz in range(sectors):
            for tt in range(terms):
                flips = home if zz // 2 == tt else away
                if flips is None:
                    continue
                flip_sector, flip_term, flip_sub = flips
                for uu in range(subs):
                    pairs.append((index(zz, tt, uu), index(zz ^ flip_sector, tt ^ flip_term, uu ^ flip_sub)))
        return lax.ppermute(value, LINE, pairs)

    def over_term(value):
        return permute(value, (0, 1, 0), (0, 1, 0))

    def over_core(value):
        return permute(value, (0, 0, 1), (0, 0, 1))

    own_same = lax.dynamic_index_in_dim(wavefunction[0], odd, 0, keepdims=False)
    other_same = over_term(own_same)
    later_odd, _ = lax.optimization_barrier((odd, own_same))
    own_flip = lax.dynamic_index_in_dim(wavefunction[0], 1 - later_odd, 0, keepdims=False)
    second_flip = own_flip
    other_flip = over_term(second_flip)
    live = live_states(right_dims, z, states)
    right = jnp.where(live[:, None] & live[None, :], right_env[0, 0], jnp.zeros((), BF16))
    right = lax.optimization_barrier(right)
    moved_first = contract(own_same, right)
    same_first = permute(moved_first, (0, 0, 0), (2, 1, 0))
    other_same, _ = lax.optimization_barrier((other_same, moved_first))
    moved_same = contract(other_same, right)
    same_second = permute(moved_same, (2, 0, 0), (0, 1, 0))
    later_u, _ = lax.optimization_barrier((u, moved_first))
    own_rows = lax.dynamic_slice_in_dim(left_env[0, 0], later_u * half, half, 0)
    other_rows = over_term(own_rows)
    early_flip, _ = lax.optimization_barrier((own_flip, moved_same))
    moved_flip = contract(early_flip, right)
    flip_first = permute(moved_flip, (1, 0, 0), (3, 1, 0))
    other_flip, _, _ = lax.optimization_barrier((other_flip, moved_flip, own_rows))
    moved_last = contract(other_flip, right)
    flip_second = permute(moved_last, (3, 0, 0), (1, 1, 0))
    cols_live = live_states(left_dims, z, states)
    rows_live = lax.dynamic_slice_in_dim(cols_live, u * half, half)
    lefts = []
    for rows in (jnp.where(at_home, own_rows, other_rows), jnp.where(at_home, other_rows, own_rows)):
        rows = jnp.where(rows_live[:, None] & cols_live[None, :], rows, jnp.zeros((), BF16))
        lefts.append([lax.dynamic_slice_in_dim(rows, part * half, half, 1) for part in (u, 1 - u)])

    def apply_left(left, mine):
        return jnp.dot(left[0], mine, preferred_element_type=F32) + jnp.dot(
            left[1], over_core(mine), preferred_element_type=F32
        )

    same = apply_left(lefts[0], same_first)
    flip = apply_left(lefts[0], flip_first)
    same = (same + apply_left(lefts[1], same_second)).astype(BF16)
    flip, flip_second, same = lax.optimization_barrier((flip, flip_second, same))
    flip = (flip + apply_left(lefts[1], flip_second)).astype(BF16)
    product = jnp.zeros((1, 2, half, width), BF16)
    product = lax.dynamic_update_slice(product, same[None, None], (0, odd, 0, 0))
    return lax.dynamic_update_slice(product, flip[None, None], (0, 1 - odd, 0, 0))


def any_size(wavefunction, left_env, right_env, left_dims, right_dims):
    z, t, u = (lax.axis_index(name) for name in LINE)
    half = wavefunction.shape[2]
    left, right = masked_envs(left_env, right_env, left_dims, right_dims, z)
    rows = lax.dynamic_slice_in_dim(left, u * half, half, 0)
    blocks = lax.all_gather(wavefunction[0], "term", axis=0, tiled=True)
    moved = jnp.einsum("akj,cj->akc", blocks, right, preferred_element_type=F32).astype(BF16)
    arrived = lax.all_to_all(moved, "sector", split_axis=0, concat_axis=0, tiled=True)
    both = lax.all_gather(arrived, "sub", axis=1, tiled=True)
    partial = jnp.einsum("rk,bkc->brc", rows, both, preferred_element_type=F32)
    return lax.psum_scatter(partial, "term", scatter_dimension=0, tiled=True).astype(BF16)[None]


def solution(mesh):
    sizes = tuple(mesh.shape[name] for name in LINE)
    return jax.shard_map(
        two_by_four if sizes == (4, 2, 2) else any_size,
        mesh=mesh,
        in_specs=(
            P(("groups", "sector"), "term", "sub", None),
            P("term", ("groups", "sector"), None, None),
            P("term", ("groups", "sector"), None, None),
            P("groups"),
            P("groups"),
        ),
        out_specs=P(("groups", "sector"), "term", "sub", None),
        check_vma=False,
    )
```

```python
import jax
import jax.numpy as jnp
from jax import lax
from jax.sharding import PartitionSpec as P

LINE = ("sector", "term", "sub")
F32 = jnp.float32
BF16 = jnp.bfloat16


def masked_envs(left_env, right_env, left_dims, right_dims, sector_pos):
    states = jnp.arange(left_env.shape[-1], dtype=jnp.int32)
    left_live = states < lax.dynamic_index_in_dim(left_dims, sector_pos, 0, keepdims=False)
    right_live = states < lax.dynamic_index_in_dim(right_dims, sector_pos, 0, keepdims=False)
    left = jnp.where(left_live[:, None] & left_live[None, :], left_env[0, 0], jnp.zeros((), left_env.dtype))
    right = jnp.where(right_live[:, None] & right_live[None, :], right_env[0, 0], jnp.zeros((), right_env.dtype))
    return left, right


def live_states(dims, sector, states):
    places = jnp.arange(dims.shape[0], dtype=jnp.int32)
    return jnp.any((places[:, None] == sector) & (states[None, :] < dims[:, None]), axis=0)


def contract(block, right):
    return lax.dot_general(block, right, (((1,), (1,)), ((), ())), preferred_element_type=F32).astype(BF16)


def two_by_four(wavefunction, left_env, right_env, left_dims, right_dims):
    z, t, u = (lax.axis_index(name) for name in LINE)
    sectors, terms, subs = (lax.axis_size(name) for name in LINE)
    half, width = wavefunction.shape[2:]
    states = jnp.arange(width, dtype=jnp.int32)
    at_home = (z // 2) == t
    odd = z & 1

    def index(zz, tt, uu):
        return (zz * terms + tt) * subs + uu

    def permute(value, home, away):
        pairs = []
        for zz in range(sectors):
            for tt in range(terms):
                flips = home if zz // 2 == tt else away
                if flips is None:
                    continue
                flip_sector, flip_term, flip_sub = flips
                for uu in range(subs):
                    pairs.append((index(zz, tt, uu), index(zz ^ flip_sector, tt ^ flip_term, uu ^ flip_sub)))
        return lax.ppermute(value, LINE, pairs)

    def over_term(value):
        return permute(value, (0, 1, 0), (0, 1, 0))

    def over_core(value):
        return permute(value, (0, 0, 1), (0, 0, 1))

    own_same = lax.dynamic_index_in_dim(wavefunction[0], odd, 0, keepdims=False)
    other_same = over_term(own_same)
    later_odd, _ = lax.optimization_barrier((odd, own_same))
    own_flip = lax.dynamic_index_in_dim(wavefunction[0], 1 - later_odd, 0, keepdims=False)
    second_flip = own_flip
    other_flip = over_term(second_flip)
    live = live_states(right_dims, z, states)
    right = jnp.where(live[:, None] & live[None, :], right_env[0, 0], jnp.zeros((), BF16))
    right = lax.optimization_barrier(right)
    moved_first = contract(own_same, right)
    same_first = permute(moved_first, (0, 0, 0), (2, 1, 0))
    other_same, _ = lax.optimization_barrier((other_same, moved_first))
    moved_same = contract(other_same, right)
    same_second = permute(moved_same, (2, 0, 0), (0, 1, 0))
    later_u, _ = lax.optimization_barrier((u, moved_first))
    own_rows = lax.dynamic_slice_in_dim(left_env[0, 0], later_u * half, half, 0)
    other_rows = over_term(own_rows)
    early_flip, _ = lax.optimization_barrier((own_flip, moved_same))
    moved_flip = contract(early_flip, right)
    flip_first = permute(moved_flip, (1, 0, 0), (3, 1, 0))
    other_flip, _, _ = lax.optimization_barrier((other_flip, moved_flip, own_rows))
    moved_last = contract(other_flip, right)
    flip_second = permute(moved_last, (3, 0, 0), (1, 1, 0))
    cols_live = live_states(left_dims, z, states)
    rows_live = lax.dynamic_slice_in_dim(cols_live, u * half, half)
    lefts = []
    for rows in (jnp.where(at_home, own_rows, other_rows), jnp.where(at_home, other_rows, own_rows)):
        rows = jnp.where(rows_live[:, None] & cols_live[None, :], rows, jnp.zeros((), BF16))
        lefts.append([lax.dynamic_slice_in_dim(rows, part * half, half, 1) for part in (u, 1 - u)])

    def apply_left(left, mine):
        return jnp.dot(left[0], mine, preferred_element_type=F32) + jnp.dot(
            left[1], over_core(mine), preferred_element_type=F32
        )

    same = apply_left(lefts[0], same_first)
    flip = apply_left(lefts[0], flip_first)
    same = (same + apply_left(lefts[1], same_second)).astype(BF16)
    flip, flip_second, same = lax.optimization_barrier((flip, flip_second, same))
    theirs = over_core(flip_second)
    flip = flip + jnp.dot(lefts[1][0], flip_second, preferred_element_type=F32)
    product = lax.dynamic_update_slice(jnp.zeros((1, 2, half, width), BF16), same[None, None], (0, odd, 0, 0))
    flip, theirs, product = lax.optimization_barrier((flip, theirs, product))
    flip = (flip + jnp.dot(lefts[1][1], theirs, preferred_element_type=F32)).astype(BF16)
    return lax.dynamic_update_slice(product, flip[None, None], (0, 1 - odd, 0, 0))


def any_size(wavefunction, left_env, right_env, left_dims, right_dims):
    z, t, u = (lax.axis_index(name) for name in LINE)
    half = wavefunction.shape[2]
    left, right = masked_envs(left_env, right_env, left_dims, right_dims, z)
    rows = lax.dynamic_slice_in_dim(left, u * half, half, 0)
    blocks = lax.all_gather(wavefunction[0], "term", axis=0, tiled=True)
    moved = jnp.einsum("akj,cj->akc", blocks, right, preferred_element_type=F32).astype(BF16)
    arrived = lax.all_to_all(moved, "sector", split_axis=0, concat_axis=0, tiled=True)
    both = lax.all_gather(arrived, "sub", axis=1, tiled=True)
    partial = jnp.einsum("rk,bkc->brc", rows, both, preferred_element_type=F32)
    return lax.psum_scatter(partial, "term", scatter_dimension=0, tiled=True).astype(BF16)[None]


def solution(mesh):
    sizes = tuple(mesh.shape[name] for name in LINE)
    return jax.shard_map(
        two_by_four if sizes == (4, 2, 2) else any_size,
        mesh=mesh,
        in_specs=(
            P(("groups", "sector"), "term", "sub", None),
            P("term", ("groups", "sector"), None, None),
            P("term", ("groups", "sector"), None, None),
            P("groups"),
            P("groups"),
        ),
        out_specs=P(("groups", "sector"), "term", "sub", None),
        check_vma=False,
    )
```

```python
import jax
import jax.numpy as jnp
from jax import lax
from jax.sharding import PartitionSpec as P

LINE = ("sector", "term", "sub")
F32 = jnp.float32
BF16 = jnp.bfloat16


def masked_envs(left_env, right_env, left_dims, right_dims, sector_pos):
    states = jnp.arange(left_env.shape[-1], dtype=jnp.int32)
    left_live = states < lax.dynamic_index_in_dim(left_dims, sector_pos, 0, keepdims=False)
    right_live = states < lax.dynamic_index_in_dim(right_dims, sector_pos, 0, keepdims=False)
    left = jnp.where(left_live[:, None] & left_live[None, :], left_env[0, 0], jnp.zeros((), left_env.dtype))
    right = jnp.where(right_live[:, None] & right_live[None, :], right_env[0, 0], jnp.zeros((), right_env.dtype))
    return left, right


def live_states(dims, sector, states):
    places = jnp.arange(dims.shape[0], dtype=jnp.int32)
    return jnp.any((places[:, None] == sector) & (states[None, :] < dims[:, None]), axis=0)


def contract(block, right):
    return lax.dot_general(block, right, (((1,), (1,)), ((), ())), preferred_element_type=F32).astype(BF16)


def two_by_four(wavefunction, left_env, right_env, left_dims, right_dims):
    z, t, u = (lax.axis_index(name) for name in LINE)
    sectors, terms, subs = (lax.axis_size(name) for name in LINE)
    half, width = wavefunction.shape[2:]
    states = jnp.arange(width, dtype=jnp.int32)
    at_home = (z // 2) == t
    odd = z & 1

    def index(zz, tt, uu):
        return (zz * terms + tt) * subs + uu

    def permute(value, home, away):
        pairs = []
        for zz in range(sectors):
            for tt in range(terms):
                flips = home if zz // 2 == tt else away
                if flips is None:
                    continue
                flip_sector, flip_term, flip_sub = flips
                for uu in range(subs):
                    pairs.append((index(zz, tt, uu), index(zz ^ flip_sector, tt ^ flip_term, uu ^ flip_sub)))
        return lax.ppermute(value, LINE, pairs)

    def over_term(value):
        return permute(value, (0, 1, 0), (0, 1, 0))

    def over_core(value):
        return permute(value, (0, 0, 1), (0, 0, 1))

    own_same = lax.dynamic_index_in_dim(wavefunction[0], odd, 0, keepdims=False)
    other_same = over_term(own_same)
    later_odd = odd
    own_flip = lax.dynamic_index_in_dim(wavefunction[0], 1 - later_odd, 0, keepdims=False)
    second_flip = own_flip
    other_flip = over_term(second_flip)
    live = live_states(right_dims, z, states)
    right = jnp.where(live[:, None] & live[None, :], right_env[0, 0], jnp.zeros((), BF16))
    right = lax.optimization_barrier(right)
    moved_first = contract(own_same, right)
    same_first = permute(moved_first, (0, 0, 0), (2, 1, 0))
    other_same, _ = lax.optimization_barrier((other_same, moved_first))
    moved_same = contract(other_same, right)
    same_second = permute(moved_same, (2, 0, 0), (0, 1, 0))
    early_flip, _ = lax.optimization_barrier((own_flip, moved_same))
    moved_flip = contract(early_flip, right)
    flip_first = permute(moved_flip, (1, 0, 0), (3, 1, 0))
    other_flip, _, _ = lax.optimization_barrier((other_flip, moved_same, moved_flip))
    moved_last = contract(other_flip, right)
    flip_second = permute(moved_last, (3, 0, 0), (1, 1, 0))
    later_u, _ = lax.optimization_barrier((u, moved_last))
    own_rows = lax.dynamic_slice_in_dim(left_env[0, 0], later_u * half, half, 0)
    other_rows = over_term(own_rows)
    cols_live = live_states(left_dims, z, states)
    rows_live = lax.dynamic_slice_in_dim(cols_live, u * half, half)
    lefts = []
    for rows in (jnp.where(at_home, own_rows, other_rows), jnp.where(at_home, other_rows, own_rows)):
        rows = jnp.where(rows_live[:, None] & cols_live[None, :], rows, jnp.zeros((), BF16))
        lefts.append([lax.dynamic_slice_in_dim(rows, part * half, half, 1) for part in (u, 1 - u)])

    def apply_left(left, mine):
        return jnp.dot(left[0], mine, preferred_element_type=F32) + jnp.dot(
            left[1], over_core(mine), preferred_element_type=F32
        )

    same = apply_left(lefts[0], same_first)
    flip = apply_left(lefts[0], flip_first)
    same = (same + apply_left(lefts[1], same_second)).astype(BF16)
    flip, flip_second, same = lax.optimization_barrier((flip, flip_second, same))
    theirs = over_core(flip_second)
    flip = flip + jnp.dot(lefts[1][0], flip_second, preferred_element_type=F32)
    flip, theirs = lax.optimization_barrier((flip, theirs))
    flip = (flip + jnp.dot(lefts[1][1], theirs, preferred_element_type=F32)).astype(BF16)
    product = jnp.zeros((1, 2, half, width), BF16)
    product = lax.dynamic_update_slice(product, same[None, None], (0, odd, 0, 0))
    return lax.dynamic_update_slice(product, flip[None, None], (0, 1 - odd, 0, 0))


def any_size(wavefunction, left_env, right_env, left_dims, right_dims):
    z, t, u = (lax.axis_index(name) for name in LINE)
    half = wavefunction.shape[2]
    left, right = masked_envs(left_env, right_env, left_dims, right_dims, z)
    rows = lax.dynamic_slice_in_dim(left, u * half, half, 0)
    blocks = lax.all_gather(wavefunction[0], "term", axis=0, tiled=True)
    moved = jnp.einsum("akj,cj->akc", blocks, right, preferred_element_type=F32).astype(BF16)
    arrived = lax.all_to_all(moved, "sector", split_axis=0, concat_axis=0, tiled=True)
    both = lax.all_gather(arrived, "sub", axis=1, tiled=True)
    partial = jnp.einsum("rk,bkc->brc", rows, both, preferred_element_type=F32)
    return lax.psum_scatter(partial, "term", scatter_dimension=0, tiled=True).astype(BF16)[None]


def solution(mesh):
    sizes = tuple(mesh.shape[name] for name in LINE)
    return jax.shard_map(
        two_by_four if sizes == (4, 2, 2) else any_size,
        mesh=mesh,
        in_specs=(
            P(("groups", "sector"), "term", "sub", None),
            P("term", ("groups", "sector"), None, None),
            P("term", ("groups", "sector"), None, None),
            P("groups"),
            P("groups"),
        ),
        out_specs=P(("groups", "sector"), "term", "sub", None),
        check_vma=False,
    )
```
